512 devices in a mesh: row: 64 (over x, z_lo, core), col: 8 (over y, z_hi).
Axes of the slice: x: 4, y: 4, z: 16 (z_hi: 2, z_lo: 8; z = z_hi * 8 + z_lo), core: 2. Of those that a mesh axis runs over, the one named last changes fastest.
Arguments:
- object_slices: float32 [2, 2, 8192, 1024], P(None, None, 'row', 'col'), may hold values from -4 to 4
- probe_field: float32 [2, 128, 128], replicated, may hold values from -6 to 6
- measured: float32 [2048, 128, 128], P(('row', 'col')), may hold values from 0.5 to 4
- offsets: int32 [2048, 2], P(('row', 'col')), may hold values from 0 to 127
- counts: int32 [512], P(('row', 'col')), may hold values from 1 to 4, 1024 in all
Outputs:
- object_grad: float32 [2, 2, 8192, 1024], P(None, None, 'row', 'col')
- probe_grad: float32 [2, 128, 128], replicated
The draws below stay inside these ranges and needn't reach their ends.
Inputs may be any that keep to these rules, and one draw needn't show every extreme that they name: `counts`: live slots of each owner tile; they sum to 1024 and some tile has exactly 4.
All inputs are finite; a program needn't handle non-finite values. No bound on the sum of `counts` on one device may be relied on, other than what follows from the above.
Results may differ from the reference program's by a relative error of at most 0.0003.
Values sent between devices are 32-bit elements; how exact they have to be, the bound alone decides.
A program may use at most 64 MiB of HBM per device.

```python
import math
import jax
import jax.numpy as jnp
import numpy as np
from jax import lax

W = 128
SLICES = 2
TILE = 128
CAP = 4
NR = 8192
NC = 1024
POSITIONS = 2048
N_COL = 8
DEVICES = 512


def touch_ends(array, key, low, high):
    index_at = [jax.random.randint(jax.random.fold_in(key, axis), (), 0, length) for axis, length in enumerate(array.shape)]
    main_axis = array.shape.index(max(array.shape))
    beside = index_at[:main_axis] + [(index_at[main_axis] + 1) % array.shape[main_axis]] + index_at[main_axis + 1:]
    return array.at[tuple(index_at)].set(low).at[tuple(beside)].set(high)


def level_of(key, shape, pieces, least, top_value):
    def one(position, shards_of):
        steps = jax.random.uniform(jax.random.fold_in(jax.random.fold_in(key, 6), position), (shards_of,), jnp.float32, least / len(pieces), top_value / len(pieces))
        return jnp.repeat(jnp.exp(steps), shape[position] // shards_of).reshape((-1,) + (1,) * (len(shape) - position - 1))

    loudness = one(*pieces[0])
    for cut in pieces[1:]:
        loudness = loudness * one(*cut)
    return loudness


def length_profile(amount, total, limit, slope):
    portions = [(1 << 20) // math.isqrt(standing ** slope) + 1 for standing in range(2, amount + 1)]
    spare, given = total - limit - (amount - 1), [1] * (amount - 1)
    while spare > 0:
        free = [i for i in range(amount - 1) if given[i] < limit]
        mass, left = sum([portions[i] for i in free]), spare
        for i in free:
            more = min(limit - given[i], max(1, left * portions[i] // mass), spare)
            given[i] = given[i] + more
            spare = spare - more
    return np.array([limit] + given)


def ragged_sizes(stream_key, count, total, limit, lean):
    if count == 2:
        one = jax.random.randint(stream_key, (), max(1, total - limit), min(limit, total - 1) + 1)
        return jnp.stack([one, total - one])
    lengths = jnp.asarray(length_profile(count, total, limit, lean), jnp.int32)
    twos = (count - 1) // 2
    donor, receiver = lengths[1:1 + 2 * twos:2], lengths[2:2 + 2 * twos:2]
    room = jnp.minimum(donor - 1, limit - receiver)
    moved = jax.random.randint(jax.random.fold_in(stream_key, 1), (twos,), 0, 1 << 20) % (room + 1)
    lengths = lengths.at[1:1 + 2 * twos:2].set(donor - moved).at[2:2 + 2 * twos:2].set(receiver + moved)
    return lengths[jax.random.permutation(jax.random.fold_in(stream_key, 2), count)]


def bell_draw(own_key, dims, width, most, shards=(), kind=jnp.bfloat16):
    loudness = level_of(own_key, dims, shards, -0.22, 0.18) if shards else 1.0
    values = jax.random.normal(own_key, dims, jnp.float32) * width * loudness
    return jnp.minimum(jnp.maximum(values, -most), most).astype(kind)


def setup_inputs(seed: int = 0) -> dict:
    arg_keys = jax.random.split(jax.random.key(seed), 6)
    object_slices = bell_draw(arg_keys[0], (SLICES, 2, NR, NC), 0.7, 4.0, ((2, 64), (3, 8)), jnp.float32)
    probe_field = bell_draw(arg_keys[1], (2, W, W), 1.0, 6.0, (), jnp.float32)
    measured = jnp.clip(0.5 + 3.5 * jax.random.uniform(arg_keys[2], (POSITIONS, W, W), jnp.float32) ** level_of(arg_keys[2], (POSITIONS, W, W), ((0, 512),), -0.2, 0.2), 0.5, 4.0)
    offsets = touch_ends(jax.random.randint(arg_keys[3], (POSITIONS, 2), 0, TILE), jax.random.fold_in(arg_keys[3], 1), 0, TILE - 1).astype(jnp.int32)
    counts = ragged_sizes(arg_keys[4], DEVICES, DEVICES * CAP // 2, CAP, 2).astype(jnp.int32)
    return {"object_slices": object_slices, "probe_field": probe_field, "measured": measured, "offsets": offsets, "counts": counts}


PROP = 40.0

def propagator(extent):
    counter = jnp.arange(extent, dtype=jnp.int32)
    freq = jnp.where(counter < extent // 2, counter, counter - extent).astype(jnp.float32)
    phases = PROP * (freq[:, None] ** 2 + freq[None, :] ** 2) / (extent * extent)
    return lax.complex(jnp.cos(phases), -jnp.sin(phases))

def slot_loss(one_patch, probe_now, target):
    kernel = propagator(W)
    wave = lax.complex(probe_now[0], probe_now[1])
    for slice_index in range(SLICES):
        wave = wave * lax.complex(one_patch[slice_index, 0], one_patch[slice_index, 1])
        if slice_index < SLICES - 1:
            wave = jnp.fft.ifft2(kernel * jnp.fft.fft2(wave, norm='ortho'), norm='ortho')
    far = jnp.fft.fft2(wave, norm='ortho')
    excess = jnp.real(far) ** 2 + jnp.imag(far) ** 2 - target
    return 0.5 * jnp.sum(excess * excess)

def reference(object_slices, probe_field, measured, offsets, counts):
    taller = jnp.concatenate([object_slices, object_slices[:, :, :W, :]], axis=2)
    extended = jnp.concatenate([taller, taller[:, :, :, :W]], axis=3)
    zero_index = jnp.zeros((), jnp.int32)

    def step_slot(carried, inputs):
        grad_extended, grad_probe = carried
        target, corner, slot_id = inputs
        device = (slot_id // CAP).astype(jnp.int32)
        live_mask = jnp.where(slot_id % CAP < counts[device], 1.0, 0.0).astype(jnp.float32)
        row_base = (device // N_COL * TILE + corner[0]).astype(jnp.int32)
        col_base = (device % N_COL * TILE + corner[1]).astype(jnp.int32)
        corner_start = (zero_index, zero_index, row_base, col_base)
        one_patch = lax.dynamic_slice(extended, corner_start, (SLICES, 2, W, W))
        loss_value, pullback = jax.vjp(lambda piece, probe_now: slot_loss(piece, probe_now, target) * live_mask, one_patch, probe_field)
        grad_patch, grad_single = pullback(jnp.ones((), loss_value.dtype))
        current = lax.dynamic_slice(grad_extended, corner_start, (SLICES, 2, W, W))
        grad_extended = lax.dynamic_update_slice(grad_extended, current + grad_patch, corner_start)
        return ((grad_extended, grad_probe + grad_single), None)
    start_carry = (jnp.zeros_like(extended), jnp.zeros_like(probe_field))
    slot_ids = jnp.arange(POSITIONS, dtype=jnp.int32)
    (grad_extended, grad_probe), unused = lax.scan(step_slot, start_carry, (measured, offsets, slot_ids))
    object_grad = grad_extended[:, :, :NR, :NC]
    object_grad = object_grad.at[:, :, :W, :].add(grad_extended[:, :, NR:, :NC])
    object_grad = object_grad.at[:, :, :, :W].add(grad_extended[:, :, :NR, NC:])
    object_grad = object_grad.at[:, :, :W, :W].add(grad_extended[:, :, NR:, NC:])
    return (object_grad, grad_probe / jnp.sqrt(jnp.float32(POSITIONS)))
```

```python
import functools
import math

import jax
import jax.numpy as jnp
import ml_dtypes
import numpy as np
from jax import lax
from jax.experimental import pallas as pl
from jax.experimental.pallas import tpu as pltpu
from jax.sharding import PartitionSpec as P

PROP = 40.0
W = 128
CAP = 4
MESH = pl.DeviceIdType.MESH
F32 = jnp.float32
BF16 = jnp.bfloat16


def _tables():
    k = np.arange(W)
    dft = np.exp(-2j * np.pi * (np.outer(k, k) % W) / W) / math.sqrt(W)
    freq = np.where(k < W // 2, k, k - W).astype(np.float64)
    h = np.exp(-1j * PROP * freq**2 / (W * W))
    prop = np.conj(dft) @ (h[:, None] * dft)
    out = np.zeros((2, 6, W, W), ml_dtypes.bfloat16)
    for t, table in enumerate((prop, dft)):
        for j, part in enumerate((table.real, table.imag, -table.imag)):
            part = part.astype(np.float32)
            high = part.astype(ml_dtypes.bfloat16)
            out[t, j] = high
            out[t, 3 + j] = (part - high.astype(np.float32)).astype(ml_dtypes.bfloat16)
    return out


def _split(x):
    high = x.astype(BF16)
    return high, (x - high.astype(F32)).astype(BF16)


def _blocks(tab, conj):
    parts = []
    for base in (0, 3):
        re, im, neg = tab[base], tab[base + 1], tab[base + 2]
        if conj:
            im, neg = neg, im
        parts.append(jnp.concatenate([jnp.concatenate([re, im], 1), jnp.concatenate([neg, re], 1)], 0))
    return parts


def _two_sided(fields, tab, conj):
    n = len(fields)
    wh, wl = _blocks(tab, conj)
    vh, vl = _blocks(tab, not conj)
    stacked = jnp.concatenate([jnp.concatenate([re, im], 1) for re, im in fields], 0)
    high, low = _split(stacked)
    y = jnp.dot(
        jnp.concatenate([high, low, high], 1), jnp.concatenate([wh, wh, wl], 0), preferred_element_type=F32
    )
    beside = jnp.concatenate(
        [jnp.concatenate([y[s * W : (s + 1) * W, :W], y[s * W : (s + 1) * W, W:]], 0) for s in range(n)], 1
    )
    high, low = _split(beside)
    z = jnp.dot(
        jnp.concatenate([vh, vh, vl], 1), jnp.concatenate([high, low, high], 0), preferred_element_type=F32
    )
    return [(z[:W, s * W : (s + 1) * W], z[W:, s * W : (s + 1) * W]) for s in range(n)]


def _mul(a, b):
    return a[0] * b[0] - a[1] * b[1], a[0] * b[1] + a[1] * b[0]


def _mul_conj(a, b):
    return a[0] * b[0] + a[1] * b[1], a[1] * b[0] - a[0] * b[1]


def _xor(i, k):
    if k == 0:
        return i
    if k == 1:
        return i + 1 - 2 * lax.rem(i, 2)
    if k == 2:
        return lax.rem(i + 2, 4)
    return 3 - i


def _kernel(
    n_row, n_col, offs, cnt, obj, probe_hbm, meas_hbm, tab_hbm, out, pout,
    own, right, below, diag, g_own, g_right, g_below, g_diag, r_right, r_below, r_diag,
    probe, meas, tab, gp, core_in, xy_in, za_in, zb_in, plane,
    local, fc_s, fc_r, fr_s, fr_r, fd_s, fd_r, bb_s, bb_r, bd_s, bd_r, bc_s, bc_r,
    core_s, core_r, xy_s, xy_r, za_s, za_r, zb_s, zb_r, ag_s, ag_r, cg_s, cg_r,
):
    row, col = lax.axis_index("row"), lax.axis_index("col")
    core = lax.rem(row, 2)
    z_lo = lax.rem(row // 2, 8)
    x = row // 16
    z_hi = lax.rem(col, 2)
    y = col // 2

    def at(x_, y_, zl, zh, core_):
        return ((x_ * 8 + zl) * 2 + core_, y_ * 2 + zh)

    up = (lax.rem(row + n_row - 1, n_row), col)
    down = (lax.rem(row + 1, n_row), col)
    lft = (row, lax.rem(col + n_col - 1, n_col))
    rgt = (row, lax.rem(col + 1, n_col))
    partner = at(x, y, z_lo, z_hi, 1 - core)
    xy_peers = [
        (_xor(x, k // 4), _xor(y, k % 4)) for k in range(16)
    ]
    za_peers = [at(x, y, (z_lo // 4) * 4 + _xor(lax.rem(z_lo, 4), k), z_hi, core) for k in range(4)]
    zb_peers = [
        at(x, y, lax.rem(z_lo + 4 * (k % 2), 8), z_hi if k < 2 else 1 - z_hi, core) for k in range(4)
    ]
    peers = [up, down, lft, rgt, partner]
    peers += [at(px, py, z_lo, z_hi, core) for px, py in xy_peers[1:]]
    peers += za_peers[1:] + zb_peers[1:]
    barrier = pltpu.get_barrier_semaphore()
    for peer in peers:
        pl.semaphore_signal(barrier, inc=1, device_id=peer, device_id_type=MESH)

    loads = [
        pltpu.make_async_copy(obj, own, local.at[0]),
        pltpu.make_async_copy(probe_hbm, probe, local.at[1]),
        pltpu.make_async_copy(meas_hbm, meas, local.at[2]),
        pltpu.make_async_copy(tab_hbm, tab, local.at[3]),
    ]
    for load in loads:
        load.start()

    def send(src, dst, s, r, to):
        copy = pltpu.make_async_remote_copy(
            src_ref=src, dst_ref=dst, send_sem=s, recv_sem=r, device_id=to, device_id_type=MESH
        )
        copy.start()
        return copy

    pl.semaphore_wait(barrier, len(peers))

    f_col = [send(obj.at[p], right.at[p], fc_s.at[p], fc_r.at[p], lft) for p in range(4)]
    f_row = [send(obj.at[p], below.at[p], fr_s.at[p], fr_r.at[p], up) for p in range(4)]
    f_diag = [None] * 4

    def pass_on(p):
        f_col[p].wait_recv()
        f_diag[p] = send(right.at[p], diag.at[p], fd_s.at[p], fd_r.at[p], up)

    rows_of = lax.broadcasted_iota(jnp.int32, (W, W), 0)
    cols_of = lax.broadcasted_iota(jnp.int32, (W, W), 1)
    corners = [(offs[s, 0], offs[s, 1]) for s in range(CAP)]
    in_own_row = [rows_of >= r for r, _ in corners]
    in_own_col = [cols_of >= c for _, c in corners]

    for load in loads:
        load.wait()
    waves = [
        tuple(pltpu.roll(pltpu.roll(probe[j], r, 0), c, 1) for j in range(2)) for r, c in corners
    ]

    def window(p, s):
        top = jnp.where(in_own_col[s], own[p], right[p])
        low = jnp.where(in_own_col[s], below[p], diag[p])
        return jnp.where(in_own_row[s], top, low)

    def arrive(p):
        f_row[p].wait_recv()
        f_diag[p].wait_recv()

    pass_on(0)
    pass_on(1)
    arrive(0)
    arrive(1)
    patch1 = [(window(0, s), window(1, s)) for s in range(CAP)]
    moved = _two_sided([_mul(waves[s], patch1[s]) for s in range(CAP)], tab.at[0], False)
    pass_on(2)
    pass_on(3)
    arrive(2)
    arrive(3)
    patch2 = [(window(2, s), window(3, s)) for s in range(CAP)]
    far = _two_sided([_mul(moved[s], patch2[s]) for s in range(CAP)], tab.at[1], False)
    live_count = cnt[0]
    back = []
    for s in range(CAP):
        re, im = far[s]
        live = jnp.where(live_count > s, 2.0, 0.0).astype(F32)
        excess = (re * re + im * im - meas[s]) * live
        back.append((re * excess, im * excess))
    back = _two_sided(back, tab.at[1], True)

    def spread(p, grads):
        parts = [jnp.zeros((W, W), F32)] * 4
        for s in range(CAP):
            top = jnp.where(in_own_row[s], grads[s], 0.0)
            low = jnp.where(in_own_row[s], 0.0, grads[s])
            parts[0] += jnp.where(in_own_col[s], top, 0.0)
            parts[1] += jnp.where(in_own_col[s], 0.0, top)
            parts[2] += jnp.where(in_own_col[s], low, 0.0)
            parts[3] += jnp.where(in_own_col[s], 0.0, low)
        g_own[p], g_right[p], g_below[p], g_diag[p] = parts

    b_below, b_diag, b_col = [None] * 4, [None] * 4, [None] * 4

    def send_down(p):
        b_diag[p] = send(g_diag.at[p], r_diag.at[p], bd_s.at[p], bd_r.at[p], down)
        b_below[p] = send(g_below.at[p], r_below.at[p], bb_s.at[p], bb_r.at[p], down)

    def send_right(p):
        b_diag[p].wait_recv()
        g_right[p] += r_diag[p]
        b_col[p] = send(g_right.at[p], r_right.at[p], bc_s.at[p], bc_r.at[p], rgt)

    grads = [_mul_conj(back[s], moved[s]) for s in range(CAP)]
    for j in range(2):
        spread(2 + j, [g[j] for g in grads])
        send_down(2 + j)
    back = _two_sided([_mul_conj(back[s], patch2[s]) for s in range(CAP)], tab.at[0], True)
    send_right(2)
    send_right(3)
    grads = [_mul_conj(back[s], waves[s]) for s in range(CAP)]
    for j in range(2):
        spread(j, [g[j] for g in grads])
        send_down(j)
    probe_grads = [_mul_conj(back[s], patch1[s]) for s in range(CAP)]
    for j in range(2):
        total = jnp.zeros((W, W), F32)
        for s, (r, c) in enumerate(corners):
            total += pltpu.roll(pltpu.roll(probe_grads[s][j], lax.rem(W - r, W), 0), lax.rem(W - c, W), 1)
        gp[j] = total

    to_core = send(gp.at[1 - core], core_in, core_s, core_r, partner)
    send_right(0)
    send_right(1)
    to_core.wait_recv()
    gp[core] += core_in[...]
    piece = x * 4 + y
    to_xy = []
    for k in range(1, 16):
        px, py = xy_peers[k]
        start = pl.multiple_of((px * 4 + py) * 8, 8)
        to_xy.append(
            send(gp.at[core, pl.ds(start, 8)], xy_in.at[k], xy_s.at[k], xy_r.at[k], at(px, py, z_lo, z_hi, core))
        )
    mine = pl.multiple_of(piece * 8, 8)
    total = gp[core, pl.ds(mine, 8)]
    for k in range(1, 16):
        to_xy[k - 1].wait_recv()
        total += xy_in[k]
    za_in[0] = total
    to_za = [send(za_in.at[0], za_in.at[k], za_s.at[k], za_r.at[k], za_peers[k]) for k in range(1, 4)]
    for copy in to_za:
        copy.wait_recv()
    zb_in[0] = (za_in[0] + za_in[1]) + (za_in[2] + za_in[3])
    to_zb = [send(zb_in.at[0], zb_in.at[k], zb_s.at[k], zb_r.at[k], zb_peers[k]) for k in range(1, 4)]
    for copy in to_zb:
        copy.wait_recv()
    total = (zb_in[0] + zb_in[1]) + (zb_in[2] + zb_in[3])
    plane[core, pl.ds(mine, 8)] = total * (1.0 / math.sqrt(n_row * n_col * CAP))
    to_ag = []
    for k in range(1, 16):
        px, py = xy_peers[k]
        to_ag.append(
            send(
                plane.at[core, pl.ds(mine, 8)], plane.at[core, pl.ds(mine, 8)], ag_s.at[k], ag_r.at[k],
                at(px, py, z_lo, z_hi, core),
            )
        )
    for copy in to_ag:
        copy.wait_recv()
    to_cg = send(plane.at[core], plane.at[core], cg_s, cg_r, partner)

    for p in (2, 3, 0, 1):
        b_below[p].wait_recv()
        g_own[p] += r_below[p]
    for p in (2, 3, 0, 1):
        b_col[p].wait_recv()
        out[p] = g_own[p] + r_right[p]
    to_cg.wait_recv()
    pout[...] = plane[...]
    for copy in f_col + f_row + f_diag + b_below + b_diag + b_col + to_xy + to_za + to_zb + to_ag + [to_core, to_cg]:
        copy.wait_send()


def _per_device(n_row, n_col, object_slices, probe_field, measured, offsets, counts):
    obj = object_slices.reshape(4, W, W)
    dma = pltpu.SemaphoreType.DMA
    tile = pltpu.VMEM((4, W, W), F32)
    any_, vmem, smem = (pl.BlockSpec(memory_space=m) for m in (pl.ANY, pltpu.VMEM, pltpu.SMEM))
    out, pout = pl.pallas_call(
        functools.partial(_kernel, n_row, n_col),
        out_shape=(jax.ShapeDtypeStruct((4, W, W), F32), jax.ShapeDtypeStruct((2, W, W), F32)),
        in_specs=[smem, smem, any_, any_, any_, any_],
        out_specs=(vmem, vmem),
        scratch_shapes=[tile] * 11
        + [
            pltpu.VMEM((2, W, W), F32),
            pltpu.VMEM((CAP, W, W), F32),
            pltpu.VMEM((2, 6, W, W), BF16),
            pltpu.VMEM((2, W, W), F32),
            pltpu.VMEM((W, W), F32),
            pltpu.VMEM((16, 8, W), F32),
            pltpu.VMEM((4, 8, W), F32),
            pltpu.VMEM((4, 8, W), F32),
            pltpu.VMEM((2, W, W), F32),
        ]
        + [dma((4,))] * 13
        + [dma, dma]
        + [dma((16,))] * 2
        + [dma((4,))] * 4
        + [dma((16,))] * 2
        + [dma, dma],
        compiler_params=pltpu.CompilerParams(
            collective_id=0, has_side_effects=True, vmem_limit_bytes=40 * 1024 * 1024
        ),
    )(offsets, counts, obj, probe_field, measured, jnp.asarray(_tables()))
    return out.reshape(object_slices.shape), pout


def solution(mesh):
    in_specs = (
        P(None, None, "row", "col"),
        P(),
        P(("row", "col"), None, None),
        P(("row", "col"), None),
        P(("row", "col")),
    )
    out_specs = (P(None, None, "row", "col"), P())
    return jax.shard_map(
        functools.partial(_per_device, mesh.shape["row"], mesh.shape["col"]),
        mesh=mesh,
        in_specs=in_specs,
        out_specs=out_specs,
        check_vma=False,
    )
```

```python
import functools
import math

import jax
import jax.numpy as jnp
import ml_dtypes
import numpy as np
from jax import lax
from jax.experimental import pallas as pl
from jax.experimental.pallas import tpu as pltpu
from jax.sharding import PartitionSpec as P

PROP = 40.0
W = 128
CAP = 4
SPLIT = 2
PARTS = 4 * SPLIT
AHEAD = 8
MESH = pl.DeviceIdType.MESH
F32 = jnp.float32
BF16 = jnp.bfloat16


def _tables():
    k = np.arange(W)
    dft = np.exp(-2j * np.pi * (np.outer(k, k) % W) / W) / math.sqrt(W)
    freq = np.where(k < W // 2, k, k - W).astype(np.float64)
    h = np.exp(-1j * PROP * freq**2 / (W * W))
    prop = np.conj(dft) @ (h[:, None] * dft)
    out = np.zeros((2, 6, W, W), ml_dtypes.bfloat16)
    for t, table in enumerate((prop, dft)):
        for j, part in enumerate((table.real, table.imag, -table.imag)):
            part = part.astype(np.float32)
            high = part.astype(ml_dtypes.bfloat16)
            out[t, j] = high
            out[t, 3 + j] = (part - high.astype(np.float32)).astype(ml_dtypes.bfloat16)
    return out


def _split(x):
    high = x.astype(BF16)
    return high, (x - high.astype(F32)).astype(BF16)


def _blocks(tab, conj):
    parts = []
    for base in (0, 3):
        re, im, neg = tab[base], tab[base + 1], tab[base + 2]
        if conj:
            im, neg = neg, im
        parts.append(jnp.concatenate([jnp.concatenate([re, im], 1), jnp.concatenate([neg, re], 1)], 0))
    return parts


def _two_sided(fields, tab, conj):
    n = len(fields)
    wh, wl = _blocks(tab, conj)
    vh, vl = _blocks(tab, not conj)
    stacked = jnp.concatenate([jnp.concatenate([re, im], 1) for re, im in fields], 0)
    high, low = _split(stacked)
    y = jnp.dot(
        jnp.concatenate([high, low, high], 1), jnp.concatenate([wh, wh, wl], 0), preferred_element_type=F32
    )
    beside = jnp.concatenate(
        [jnp.concatenate([y[s * W : (s + 1) * W, :W], y[s * W : (s + 1) * W, W:]], 0) for s in range(n)], 1
    )
    high, low = _split(beside)
    z = jnp.dot(
        jnp.concatenate([vh, vh, vl], 1), jnp.concatenate([high, low, high], 0), preferred_element_type=F32
    )
    return [(z[:W, s * W : (s + 1) * W], z[W:, s * W : (s + 1) * W]) for s in range(n)]


def _mul(a, b):
    return a[0] * b[0] - a[1] * b[1], a[0] * b[1] + a[1] * b[0]


def _mul_conj(a, b):
    return a[0] * b[0] + a[1] * b[1], a[1] * b[0] - a[0] * b[1]


def _xor(i, k):
    if k == 0:
        return i
    if k == 1:
        return i + 1 - 2 * lax.rem(i, 2)
    if k == 2:
        return lax.rem(i + 2, 4)
    return 3 - i


def _kernel(
    n_row, n_col, offs, cnt, obj, probe_hbm, meas_hbm, tab_hbm, out, pout,
    own, right, below, diag, g_own, g_right, g_below, g_diag, r_right, r_below, r_diag,
    probe, meas, tab, gp, core_in, xy_in, z_in, plane,
    local, fc_s, fc_r, fr_s, fr_r, fd_s, fd_r, bb_s, bb_r, bd_s, bd_r, bc_s, bc_r,
    core_s, core_r, xy_s, xy_r, z_s, z_r, ag_s, ag_r, cg_s, cg_r,
):
    row, col = lax.axis_index("row"), lax.axis_index("col")
    core = lax.rem(row, 2)
    z_lo = lax.rem(row // 2, 8)
    x = row // 16
    z_hi = lax.rem(col, 2)
    y = col // 2
    first, last = lax.rem(row, 16) == 0, lax.rem(row, 16) == 15

    def at(x_, y_, zl, zh, core_):
        return ((x_ * 8 + zl) * 2 + core_, y_ * 2 + zh)

    row_up, row_down = lax.rem(row + n_row - 1, n_row), lax.rem(row + 1, n_row)
    col_left, col_right = lax.rem(col + n_col - 1, n_col), lax.rem(col + 1, n_col)
    up, down, lft, rgt = (row_up, col), (row_down, col), (row, col_left), (row, col_right)
    up_left, down_right = (row_up, col_left), (row_down, col_right)
    partner = at(x, y, z_lo, z_hi, 1 - core)
    xy_peers = [(_xor(x, k // 4), _xor(y, k % 4)) for k in range(16)]
    z = z_hi * 8 + z_lo
    z_peers = []
    for k in range(16):
        other = lax.rem(z + k, 16)
        z_peers.append(at(x, y, lax.rem(other, 8), other // 8, core))
    peers = [up, down, lft, rgt, partner, up_left, down_right]
    peers += [at(px, py, z_lo, z_hi, core) for px, py in xy_peers[1:]]
    peers += z_peers[1:]
    barrier = pltpu.get_barrier_semaphore()
    for peer in peers:
        pl.semaphore_signal(barrier, inc=1, device_id=peer, device_id_type=MESH)

    loads = [
        pltpu.make_async_copy(obj, own, local.at[0]),
        pltpu.make_async_copy(probe_hbm, probe, local.at[1]),
        pltpu.make_async_copy(meas_hbm, meas, local.at[2]),
        pltpu.make_async_copy(tab_hbm, tab, local.at[3]),
    ]
    for load in loads:
        load.start()

    def remote(src, dst, s, r, to):
        return pltpu.make_async_remote_copy(
            src_ref=src, dst_ref=dst, send_sem=s, recv_sem=r, device_id=to, device_id_type=MESH
        )

    def send(src, dst, s, r, to):
        copy = remote(src, dst, s, r, to)
        copy.start()
        return copy

    pl.semaphore_wait(barrier, len(peers))

    def part(ref, i):
        return ref.at[i // SPLIT, pl.ds((i % SPLIT) * (W // SPLIT), W // SPLIT)]

    def send_left(i):
        return send(part(obj, i), part(right, i), fc_s.at[i], fc_r.at[i], lft)

    f_col = [send_left(i) for i in range(AHEAD)]
    f_row = [send(obj.at[p], below.at[p], fr_s.at[p], fr_r.at[p], up) for p in range(4)]
    f_diag = [remote(part(right, i), part(diag, i), fd_s.at[i], fd_r.at[i], up) for i in range(PARTS)]

    @pl.when(first)
    def _():
        for i in range(PARTS):
            send(part(obj, i), part(diag, i), fd_s.at[i], fd_r.at[i], up_left)

    def pass_on(i):
        f_col[i].wait_recv()

        @pl.when(jnp.logical_not(first))
        def _():
            f_diag[i].start()

        if i + AHEAD < PARTS:
            f_col[i].wait_send()
            f_col.append(send_left(i + AHEAD))

    rows_of = lax.broadcasted_iota(jnp.int32, (W, W), 0)
    cols_of = lax.broadcasted_iota(jnp.int32, (W, W), 1)
    corners = [(offs[0, s], offs[1, s]) for s in range(CAP)]
    in_own_row = [rows_of >= r for r, _ in corners]
    in_own_col = [cols_of >= c for _, c in corners]

    for load in loads:
        load.wait()
    waves = [
        tuple(pltpu.roll(pltpu.roll(probe[j], r, 0), c, 1) for j in range(2)) for r, c in corners
    ]

    def window(p, s):
        top = jnp.where(in_own_col[s], own[p], right[p])
        low = jnp.where(in_own_col[s], below[p], diag[p])
        return jnp.where(in_own_row[s], top, low)

    def arrive(p):
        f_row[p].wait_recv()
        for i in range(p * SPLIT, (p + 1) * SPLIT):
            f_diag[i].wait_recv()

    early = 2 * SPLIT + 1
    for i in range(early):
        pass_on(i)
    arrive(0)
    arrive(1)
    patch1 = [(window(0, s), window(1, s)) for s in range(CAP)]
    moved = _two_sided([_mul(waves[s], patch1[s]) for s in range(CAP)], tab.at[0], False)
    for i in range(early, PARTS):
        pass_on(i)
    arrive(2)
    arrive(3)
    patch2 = [(window(2, s), window(3, s)) for s in range(CAP)]
    far = _two_sided([_mul(moved[s], patch2[s]) for s in range(CAP)], tab.at[1], False)
    live_count = cnt[0]
    back = []
    for s in range(CAP):
        re, im = far[s]
        live = jnp.where(live_count > s, 2.0, 0.0).astype(F32)
        excess = (re * re + im * im - meas[s]) * live
        back.append((re * excess, im * excess))
    back = _two_sided(back, tab.at[1], True)

    def spread(p, grads):
        parts = [jnp.zeros((W, W), F32)] * 4
        for s in range(CAP):
            top = jnp.where(in_own_row[s], grads[s], 0.0)
            low = jnp.where(in_own_row[s], 0.0, grads[s])
            parts[0] += jnp.where(in_own_col[s], top, 0.0)
            parts[1] += jnp.where(in_own_col[s], 0.0, top)
            parts[2] += jnp.where(in_own_col[s], low, 0.0)
            parts[3] += jnp.where(in_own_col[s], 0.0, low)
        g_own[p], g_right[p], g_below[p], g_diag[p] = parts

    b_diag = [remote(g_diag.at[p], r_diag.at[p], bd_s.at[p], bd_r.at[p], down) for p in range(4)]
    b_below, b_col = [None] * 4, [None] * 4

    def send_diag(p):
        @pl.when(jnp.logical_not(last))
        def _():
            b_diag[p].start()

        @pl.when(last)
        def _():
            send(g_diag.at[p], r_diag.at[p], bd_s.at[p], bd_r.at[p], down_right)

    def send_below(p):
        b_below[p] = send(g_below.at[p], r_below.at[p], bb_s.at[p], bb_r.at[p], down)

    def send_right(p):
        @pl.when(jnp.logical_not(first))
        def _():
            b_diag[p].wait_recv()
            g_right[p] += r_diag[p]

        b_col[p] = send(g_right.at[p], r_right.at[p], bc_s.at[p], bc_r.at[p], rgt)

    grads = [_mul_conj(back[s], moved[s]) for s in range(CAP)]
    for j in range(2):
        spread(2 + j, [g[j] for g in grads])
        send_diag(2 + j)
    back = _two_sided([_mul_conj(back[s], patch2[s]) for s in range(CAP)], tab.at[0], True)
    grads = [_mul_conj(back[s], waves[s]) for s in range(CAP)]
    for j in range(2):
        spread(j, [g[j] for g in grads])
        send_diag(j)
    send_right(2)
    send_right(3)
    probe_grads = [_mul_conj(back[s], patch1[s]) for s in range(CAP)]
    for j in range(2):
        total = jnp.zeros((W, W), F32)
        for s, (r, c) in enumerate(corners):
            total += pltpu.roll(pltpu.roll(probe_grads[s][j], lax.rem(W - r, W), 0), lax.rem(W - c, W), 1)
        gp[j] = total

    for p in (2, 3, 0, 1):
        send_below(p)
    to_core = send(gp.at[1 - core], core_in, core_s, core_r, partner)
    to_core.wait_recv()
    gp[core] += core_in[...]
    mine = pl.multiple_of((x * 4 + y) * 8, 8)
    to_xy = []
    for k in (1, 2, 3, 4, 5, 6, 7, 8, 9, 10, 11, 12, 13, 14, 15):
        px, py = xy_peers[k]
        start = pl.multiple_of((px * 4 + py) * 8, 8)
        to_xy.append(send(gp.at[core, pl.ds(start, 8)], xy_in.at[k], xy_s.at[k], xy_r.at[k], at(px, py, z_lo, z_hi, core)))
    total = gp[core, pl.ds(mine, 8)]
    for k in range(1, 16):
        to_xy[k - 1].wait_recv()
    for k in range(1, 16):
        total += xy_in[k]
    z_in[z] = total
    to_z = []
    for k in (1, 2, 3, 4, 5, 6, 7, 8, 9, 10, 11, 12, 13, 14, 15):
        to_z.append(send(z_in.at[z], z_in.at[z], z_s.at[k], z_r.at[z], z_peers[k]))
    for k in range(1, 16):
        remote(z_in.at[z], z_in.at[z], z_s.at[k], z_r.at[lax.rem(z + k, 16)], z_peers[k]).wait_recv()
    total = z_in[0]
    for k in range(1, 16):
        total += z_in[k]
    plane[core, pl.ds(mine, 8)] = total * (1.0 / math.sqrt(n_row * n_col * CAP))
    send_right(0)
    send_right(1)
    to_ag = []
    for k in (1, 2, 3, 4, 5, 6, 7, 8, 9, 10, 11, 12, 13, 14, 15):
        px, py = xy_peers[k]
        held = plane.at[core, pl.ds(mine, 8)]
        to_ag.append(send(held, held, ag_s.at[k], ag_r.at[k], at(px, py, z_lo, z_hi, core)))
    for copy in to_ag:
        copy.wait_recv()
    to_cg = send(plane.at[core], plane.at[core], cg_s, cg_r, partner)

    for p in (2, 3, 0, 1):
        b_below[p].wait_recv()
        g_own[p] += r_below[p]

        @pl.when(first)
        def _():
            b_diag[p].wait_recv()
            g_own[p] += r_diag[p]

    for p in (2, 3, 0, 1):
        b_col[p].wait_recv()
        out[p] = g_own[p] + r_right[p]
    to_cg.wait_recv()
    pout[...] = plane[...]
    sent = f_col[PARTS - AHEAD :] + f_row + f_diag + b_below + b_diag + b_col
    for copy in sent + to_xy + to_z + to_ag + [to_core, to_cg]:
        copy.wait_send()


def _per_device(n_row, n_col, object_slices, probe_field, measured, offsets, counts):
    obj = object_slices.reshape(4, W, W)
    dma = pltpu.SemaphoreType.DMA
    tile = pltpu.VMEM((4, W, W), F32)
    any_, vmem, smem = (pl.BlockSpec(memory_space=m) for m in (pl.ANY, pltpu.VMEM, pltpu.SMEM))
    out, pout = pl.pallas_call(
        functools.partial(_kernel, n_row, n_col),
        out_shape=(jax.ShapeDtypeStruct((4, W, W), F32), jax.ShapeDtypeStruct((2, W, W), F32)),
        in_specs=[smem, smem, any_, any_, any_, any_],
        out_specs=(vmem, vmem),
        scratch_shapes=[tile] * 11
        + [
            pltpu.VMEM((2, W, W), F32),
            pltpu.VMEM((CAP, W, W), F32),
            pltpu.VMEM((2, 6, W, W), BF16),
            pltpu.VMEM((2, W, W), F32),
            pltpu.VMEM((W, W), F32),
            pltpu.VMEM((16, 8, W), F32),
            pltpu.VMEM((16, 8, W), F32),
            pltpu.VMEM((2, W, W), F32),
        ]
        + [dma((4,))]
        + [dma((PARTS,))] * 2
        + [dma((4,))] * 2
        + [dma((PARTS,))] * 2
        + [dma((4,))] * 6
        + [dma, dma]
        + [dma((16,))] * 6
        + [dma, dma],
        compiler_params=pltpu.CompilerParams(
            collective_id=0, has_side_effects=True, vmem_limit_bytes=60 * 1024 * 1024
        ),
    )(offsets.T, counts, obj, probe_field, measured, jnp.asarray(_tables()))
    return out.reshape(object_slices.shape), pout


def solution(mesh):
    in_specs = (
        P(None, None, "row", "col"),
        P(),
        P(("row", "col"), None, None),
        P(("row", "col"), None),
        P(("row", "col")),
    )
    out_specs = (P(None, None, "row", "col"), P())
    return jax.shard_map(
        functools.partial(_per_device, mesh.shape["row"], mesh.shape["col"]),
        mesh=mesh,
        in_specs=in_specs,
        out_specs=out_specs,
        check_vma=False,
    )
```

```python
import functools
import math

import jax
import jax.numpy as jnp
import ml_dtypes
import numpy as np
from jax import lax
from jax.experimental import pallas as pl
from jax.experimental.pallas import tpu as pltpu
from jax.sharding import PartitionSpec as P

PROP = 40.0
W = 128
CAP = 4
SPLIT = 2
PARTS = 4 * SPLIT
AHEAD = 8
MESH = pl.DeviceIdType.MESH
F32 = jnp.float32
BF16 = jnp.bfloat16


def _tables():
    k = np.arange(W)
    dft = np.exp(-2j * np.pi * (np.outer(k, k) % W) / W) / math.sqrt(W)
    freq = np.where(k < W // 2, k, k - W).astype(np.float64)
    h = np.exp(-1j * PROP * freq**2 / (W * W))
    prop = np.conj(dft) @ (h[:, None] * dft)
    out = np.zeros((2, 6, W, W), ml_dtypes.bfloat16)
    for t, table in enumerate((prop, dft)):
        for j, part in enumerate((table.real, table.imag, -table.imag)):
            part = part.astype(np.float32)
            high = part.astype(ml_dtypes.bfloat16)
            out[t, j] = high
            out[t, 3 + j] = (part - high.astype(np.float32)).astype(ml_dtypes.bfloat16)
    return out


def _split(x):
    high = x.astype(BF16)
    return high, (x - high.astype(F32)).astype(BF16)


def _blocks(tab, conj):
    parts = []
    for base in (0, 3):
        re, im, neg = tab[base], tab[base + 1], tab[base + 2]
        if conj:
            im, neg = neg, im
        parts.append(jnp.concatenate([jnp.concatenate([re, im], 1), jnp.concatenate([neg, re], 1)], 0))
    return parts


def _two_sided(fields, tab, conj):
    n = len(fields)
    wh, wl = _blocks(tab, conj)
    vh, vl = _blocks(tab, not conj)
    stacked = jnp.concatenate([jnp.concatenate([re, im], 1) for re, im in fields], 0)
    high, low = _split(stacked)
    y = jnp.dot(
        jnp.concatenate([high, low, high], 1), jnp.concatenate([wh, wh, wl], 0), preferred_element_type=F32
    )
    beside = jnp.concatenate(
        [jnp.concatenate([y[s * W : (s + 1) * W, :W], y[s * W : (s + 1) * W, W:]], 0) for s in range(n)], 1
    )
    high, low = _split(beside)
    z = jnp.dot(
        jnp.concatenate([vh, vh, vl], 1), jnp.concatenate([high, low, high], 0), preferred_element_type=F32
    )
    return [(z[:W, s * W : (s + 1) * W], z[W:, s * W : (s + 1) * W]) for s in range(n)]


def _mul(a, b):
    return a[0] * b[0] - a[1] * b[1], a[0] * b[1] + a[1] * b[0]


def _mul_conj(a, b):
    return a[0] * b[0] + a[1] * b[1], a[1] * b[0] - a[0] * b[1]


def _xor(i, k):
    if k == 0:
        return i
    if k == 1:
        return i + 1 - 2 * lax.rem(i, 2)
    if k == 2:
        return lax.rem(i + 2, 4)
    return 3 - i


def _kernel(
    n_row, n_col, offs, cnt, obj, probe_hbm, meas_hbm, tab_hbm, out, pout,
    own, right, below, diag, g_own, g_right, g_below, g_diag, r_right, r_below, r_diag,
    probe, meas, tab, gp, core_in, xy_in, z_in, plane,
    local, fc_s, fc_r, fr_s, fr_r, fd_s, fd_r, bb_s, bb_r, bd_s, bd_r, bc_s, bc_r,
    core_s, core_r, xy_s, xy_r, z_s, z_r, ag_s, ag_r, cg_s, cg_r,
):
    row, col = lax.axis_index("row"), lax.axis_index("col")
    core = lax.rem(row, 2)
    z_lo = lax.rem(row // 2, 8)
    x = row // 16
    z_hi = lax.rem(col, 2)
    y = col // 2
    first, last = lax.rem(row, 16) == 0, lax.rem(row, 16) == 15

    def at(x_, y_, zl, zh, core_):
        return ((x_ * 8 + zl) * 2 + core_, y_ * 2 + zh)

    row_up, row_down = lax.rem(row + n_row - 1, n_row), lax.rem(row + 1, n_row)
    col_left, col_right = lax.rem(col + n_col - 1, n_col), lax.rem(col + 1, n_col)
    up, down, lft, rgt = (row_up, col), (row_down, col), (row, col_left), (row, col_right)
    up_left, down_right = (row_up, col_left), (row_down, col_right)
    partner = at(x, y, z_lo, z_hi, 1 - core)
    xy_peers = [(_xor(x, k // 4), _xor(y, k % 4)) for k in range(16)]
    za_peers = [at(x, y, (z_lo // 4) * 4 + _xor(lax.rem(z_lo, 4), k), z_hi, core) for k in range(4)]
    zb_peers = [at(x, y, lax.rem(z_lo + 4 * (k % 2), 8), z_hi if k < 2 else 1 - z_hi, core) for k in range(4)]
    peers = [up, down, lft, rgt, partner, up_left, down_right]
    peers += [at(px, py, z_lo, z_hi, core) for px, py in xy_peers[1:]]
    peers += za_peers[1:] + zb_peers[1:]
    barrier = pltpu.get_barrier_semaphore()
    for peer in peers:
        pl.semaphore_signal(barrier, inc=1, device_id=peer, device_id_type=MESH)

    loads = [
        pltpu.make_async_copy(obj, own, local.at[0]),
        pltpu.make_async_copy(probe_hbm, probe, local.at[1]),
        pltpu.make_async_copy(meas_hbm, meas, local.at[2]),
        pltpu.make_async_copy(tab_hbm, tab, local.at[3]),
    ]
    for load in loads:
        load.start()

    def remote(src, dst, s, r, to):
        return pltpu.make_async_remote_copy(
            src_ref=src, dst_ref=dst, send_sem=s, recv_sem=r, device_id=to, device_id_type=MESH
        )

    def send(src, dst, s, r, to):
        copy = remote(src, dst, s, r, to)
        copy.start()
        return copy

    pl.semaphore_wait(barrier, len(peers))

    def part(ref, i):
        return ref.at[i // SPLIT, pl.ds((i % SPLIT) * (W // SPLIT), W // SPLIT)]

    def send_left(i):
        return send(part(obj, i), part(right, i), fc_s.at[i], fc_r.at[i], lft)

    f_col = [send_left(i) for i in range(AHEAD)]
    f_row = [send(obj.at[p], below.at[p], fr_s.at[p], fr_r.at[p], up) for p in range(4)]
    f_diag = [remote(part(right, i), part(diag, i), fd_s.at[i], fd_r.at[i], up) for i in range(PARTS)]

    @pl.when(first)
    def _():
        for i in range(PARTS):
            send(part(obj, i), part(diag, i), fd_s.at[i], fd_r.at[i], up_left)

    def pass_on(i):
        f_col[i].wait_recv()

        @pl.when(jnp.logical_not(first))
        def _():
            f_diag[i].start()

        if i + AHEAD < PARTS:
            f_col[i].wait_send()
            f_col.append(send_left(i + AHEAD))

    rows_of = lax.broadcasted_iota(jnp.int32, (W, W), 0)
    cols_of = lax.broadcasted_iota(jnp.int32, (W, W), 1)
    corners = [(offs[0, s], offs[1, s]) for s in range(CAP)]
    in_own_row = [rows_of >= r for r, _ in corners]
    in_own_col = [cols_of >= c for _, c in corners]

    for load in loads:
        load.wait()
    waves = [
        tuple(pltpu.roll(pltpu.roll(probe[j], r, 0), c, 1) for j in range(2)) for r, c in corners
    ]

    def window(p, s):
        top = jnp.where(in_own_col[s], own[p], right[p])
        low = jnp.where(in_own_col[s], below[p], diag[p])
        return jnp.where(in_own_row[s], top, low)

    def arrive(p):
        f_row[p].wait_recv()
        for i in range(p * SPLIT, (p + 1) * SPLIT):
            f_diag[i].wait_recv()

    early = 2 * SPLIT + 1
    for i in range(early):
        pass_on(i)
    arrive(0)
    arrive(1)
    patch1 = [(window(0, s), window(1, s)) for s in range(CAP)]
    moved = _two_sided([_mul(waves[s], patch1[s]) for s in range(CAP)], tab.at[0], False)
    for i in range(early, PARTS):
        pass_on(i)
    arrive(2)
    arrive(3)
    patch2 = [(window(2, s), window(3, s)) for s in range(CAP)]
    far = _two_sided([_mul(moved[s], patch2[s]) for s in range(CAP)], tab.at[1], False)
    live_count = cnt[0]
    back = []
    for s in range(CAP):
        re, im = far[s]
        live = jnp.where(live_count > s, 2.0, 0.0).astype(F32)
        excess = (re * re + im * im - meas[s]) * live
        back.append((re * excess, im * excess))
    back = _two_sided(back, tab.at[1], True)

    def spread(p, grads):
        parts = [jnp.zeros((W, W), F32)] * 4
        for s in range(CAP):
            top = jnp.where(in_own_row[s], grads[s], 0.0)
            low = jnp.where(in_own_row[s], 0.0, grads[s])
            parts[0] += jnp.where(in_own_col[s], top, 0.0)
            parts[1] += jnp.where(in_own_col[s], 0.0, top)
            parts[2] += jnp.where(in_own_col[s], low, 0.0)
            parts[3] += jnp.where(in_own_col[s], 0.0, low)
        g_own[p], g_right[p], g_below[p], g_diag[p] = parts

    b_diag = [remote(g_diag.at[p], r_diag.at[p], bd_s.at[p], bd_r.at[p], down) for p in range(4)]
    b_below, b_col = [None] * 4, [None] * 4

    def send_diag(p):
        @pl.when(jnp.logical_not(last))
        def _():
            b_diag[p].start()

        @pl.when(last)
        def _():
            send(g_diag.at[p], r_diag.at[p], bd_s.at[p], bd_r.at[p], down_right)

    def send_below(p):
        b_below[p] = send(g_below.at[p], r_below.at[p], bb_s.at[p], bb_r.at[p], down)

    def send_right(p):
        @pl.when(jnp.logical_not(first))
        def _():
            b_diag[p].wait_recv()
            g_right[p] += r_diag[p]

        b_col[p] = send(g_right.at[p], r_right.at[p], bc_s.at[p], bc_r.at[p], rgt)

    grads = [_mul_conj(back[s], moved[s]) for s in range(CAP)]
    for j in range(2):
        spread(2 + j, [g[j] for g in grads])
        send_diag(2 + j)
    back = _two_sided([_mul_conj(back[s], patch2[s]) for s in range(CAP)], tab.at[0], True)
    grads = [_mul_conj(back[s], waves[s]) for s in range(CAP)]
    for j in range(2):
        spread(j, [g[j] for g in grads])
        send_diag(j)
    probe_grads = [_mul_conj(back[s], patch1[s]) for s in range(CAP)]
    for j in range(2):
        total = jnp.zeros((W, W), F32)
        for s, (r, c) in enumerate(corners):
            total += pltpu.roll(pltpu.roll(probe_grads[s][j], lax.rem(W - r, W), 0), lax.rem(W - c, W), 1)
        gp[j] = total

    to_core = send(gp.at[1 - core], core_in, core_s, core_r, partner)
    to_core.wait_recv()
    gp[core] += core_in[...]
    mine = pl.multiple_of((x * 4 + y) * 8, 8)
    to_xy = []
    for k in (1, 2, 3, 4, 5, 6, 7, 8, 9, 10, 11, 12, 13, 14, 15):
        px, py = xy_peers[k]
        start = pl.multiple_of((px * 4 + py) * 8, 8)
        to_xy.append(send(gp.at[core, pl.ds(start, 8)], xy_in.at[k], xy_s.at[k], xy_r.at[k], at(px, py, z_lo, z_hi, core)))
    send_right(2)
    total = gp[core, pl.ds(mine, 8)]
    for k in range(1, 16):
        to_xy[k - 1].wait_recv()
    for k in range(1, 16):
        total += xy_in[k]
    z_in[0] = total
    to_z = [send(z_in.at[0], z_in.at[k], z_s.at[k], z_r.at[k], za_peers[k]) for k in range(1, 4)]
    send_right(3)
    for copy in to_z[:3]:
        copy.wait_recv()
    z_in[4] = (z_in[0] + z_in[1]) + (z_in[2] + z_in[3])
    to_z += [send(z_in.at[4], z_in.at[4 + k], z_s.at[4 + k], z_r.at[4 + k], zb_peers[k]) for k in range(1, 4)]
    for p in (2, 3, 0, 1):
        send_below(p)
    for copy in to_z[3:]:
        copy.wait_recv()
    total = (z_in[4] + z_in[5]) + (z_in[6] + z_in[7])
    plane[core, pl.ds(mine, 8)] = total * (1.0 / math.sqrt(n_row * n_col * CAP))
    send_right(0)
    send_right(1)
    to_ag = []
    for k in (1, 2, 3, 4, 5, 6, 7, 8, 9, 10, 11, 12, 13, 14, 15):
        px, py = xy_peers[k]
        held = plane.at[core, pl.ds(mine, 8)]
        to_ag.append(send(held, held, ag_s.at[k], ag_r.at[k], at(px, py, z_lo, z_hi, core)))
    for copy in to_ag:
        copy.wait_recv()
    to_cg = send(plane.at[core], plane.at[core], cg_s, cg_r, partner)

    for p in (2, 3, 0, 1):
        b_below[p].wait_recv()
        g_own[p] += r_below[p]

        @pl.when(first)
        def _():
            b_diag[p].wait_recv()
            g_own[p] += r_diag[p]

    for p in (2, 3, 0, 1):
        b_col[p].wait_recv()
        out[p] = g_own[p] + r_right[p]
    to_cg.wait_recv()
    pout[...] = plane[...]
    sent = f_col[PARTS - AHEAD :] + f_row + f_diag + b_below + b_diag + b_col
    for copy in sent + to_xy + to_z + to_ag + [to_core, to_cg]:
        copy.wait_send()


def _per_device(n_row, n_col, object_slices, probe_field, measured, offsets, counts):
    obj = object_slices.reshape(4, W, W)
    dma = pltpu.SemaphoreType.DMA
    tile = pltpu.VMEM((4, W, W), F32)
    any_, vmem, smem = (pl.BlockSpec(memory_space=m) for m in (pl.ANY, pltpu.VMEM, pltpu.SMEM))
    out, pout = pl.pallas_call(
        functools.partial(_kernel, n_row, n_col),
        out_shape=(jax.ShapeDtypeStruct((4, W, W), F32), jax.ShapeDtypeStruct((2, W, W), F32)),
        in_specs=[smem, smem, any_, any_, any_, any_],
        out_specs=(vmem, vmem),
        scratch_shapes=[tile] * 11
        + [
            pltpu.VMEM((2, W, W), F32),
            pltpu.VMEM((CAP, W, W), F32),
            pltpu.VMEM((2, 6, W, W), BF16),
            pltpu.VMEM((2, W, W), F32),
            pltpu.VMEM((W, W), F32),
            pltpu.VMEM((16, 8, W), F32),
            pltpu.VMEM((8, 8, W), F32),
            pltpu.VMEM((2, W, W), F32),
        ]
        + [dma((4,))]
        + [dma((PARTS,))] * 2
        + [dma((4,))] * 2
        + [dma((PARTS,))] * 2
        + [dma((4,))] * 6
        + [dma, dma]
        + [dma((16,))] * 2
        + [dma((8,))] * 2
        + [dma((16,))] * 2
        + [dma, dma],
        compiler_params=pltpu.CompilerParams(
            collective_id=0, has_side_effects=True, vmem_limit_bytes=60 * 1024 * 1024
        ),
    )(offsets.T, counts, obj, probe_field, measured, jnp.asarray(_tables()))
    return out.reshape(object_slices.shape), pout


def solution(mesh):
    in_specs = (
        P(None, None, "row", "col"),
        P(),
        P(("row", "col"), None, None),
        P(("row", "col"), None),
        P(("row", "col")),
    )
    out_specs = (P(None, None, "row", "col"), P())
    return jax.shard_map(
        functools.partial(_per_device, mesh.shape["row"], mesh.shape["col"]),
        mesh=mesh,
        in_specs=in_specs,
        out_specs=out_specs,
        check_vma=False,
    )
```

```python
import functools
import math

import jax
import jax.numpy as jnp
import ml_dtypes
import numpy as np
from jax import lax
from jax.experimental import pallas as pl
from jax.experimental.pallas import tpu as pltpu
from jax.sharding import PartitionSpec as P

PROP = 40.0
W = 128
CAP = 4
SPLIT = 2
PARTS = 4 * SPLIT
AHEAD = 8
MESH = pl.DeviceIdType.MESH
F32 = jnp.float32
BF16 = jnp.bfloat16


def _tables():
    k = np.arange(W)
    dft = np.exp(-2j * np.pi * (np.outer(k, k) % W) / W) / math.sqrt(W)
    freq = np.where(k < W // 2, k, k - W).astype(np.float64)
    h = np.exp(-1j * PROP * freq**2 / (W * W))
    prop = np.conj(dft) @ (h[:, None] * dft)
    out = np.zeros((2, 6, W, W), ml_dtypes.bfloat16)
    for t, table in enumerate((prop, dft)):
        for j, part in enumerate((table.real, table.imag, -table.imag)):
            part = part.astype(np.float32)
            high = part.astype(ml_dtypes.bfloat16)
            out[t, j] = high
            out[t, 3 + j] = (part - high.astype(np.float32)).astype(ml_dtypes.bfloat16)
    return out


def _split(x):
    high = x.astype(BF16)
    return high, (x - high.astype(F32)).astype(BF16)


def _blocks(tab, conj):
    parts = []
    for base in (0, 3):
        re, im, neg = tab[base], tab[base + 1], tab[base + 2]
        if conj:
            im, neg = neg, im
        parts.append(jnp.concatenate([jnp.concatenate([re, im], 1), jnp.concatenate([neg, re], 1)], 0))
    return parts


def _two_sided(fields, tab, conj):
    n = len(fields)
    wh, wl = _blocks(tab, conj)
    vh, vl = _blocks(tab, not conj)
    stacked = jnp.concatenate([jnp.concatenate([re, im], 1) for re, im in fields], 0)
    high, low = _split(stacked)
    y = jnp.dot(
        jnp.concatenate([high, low, high], 1), jnp.concatenate([wh, wh, wl], 0), preferred_element_type=F32
    )
    beside = jnp.concatenate(
        [jnp.concatenate([y[s * W : (s + 1) * W, :W], y[s * W : (s + 1) * W, W:]], 0) for s in range(n)], 1
    )
    high, low = _split(beside)
    z = jnp.dot(
        jnp.concatenate([vh, vh, vl], 1), jnp.concatenate([high, low, high], 0), preferred_element_type=F32
    )
    return [(z[:W, s * W : (s + 1) * W], z[W:, s * W : (s + 1) * W]) for s in range(n)]


def _mul(a, b):
    return a[0] * b[0] - a[1] * b[1], a[0] * b[1] + a[1] * b[0]


def _mul_conj(a, b):
    return a[0] * b[0] + a[1] * b[1], a[1] * b[0] - a[0] * b[1]


def _xor(i, k):
    if k == 0:
        return i
    if k == 1:
        return i + 1 - 2 * lax.rem(i, 2)
    if k == 2:
        return lax.rem(i + 2, 4)
    return 3 - i


def _kernel(
    n_row, n_col, offs, cnt, obj, probe_hbm, meas_hbm, tab_hbm, out, pout,
    own, right, below, diag, g_own, g_right, g_below, g_diag, r_right, r_below, r_diag,
    probe, meas, tab, gp, core_in, xy_in, z_in, plane,
    local, fc_s, fc_r, fr_s, fr_r, fd_s, fd_r, bb_s, bb_r, bd_s, bd_r, bc_s, bc_r,
    core_s, core_r, xy_s, xy_r, z_s, z_r, ag_s, ag_r, cg_s, cg_r,
):
    row, col = lax.axis_index("row"), lax.axis_index("col")
    core = lax.rem(row, 2)
    z_lo = lax.rem(row // 2, 8)
    x = row // 16
    z_hi = lax.rem(col, 2)
    y = col // 2
    first, last = lax.rem(row, 16) == 0, lax.rem(row, 16) == 15

    def at(x_, y_, zl, zh, core_):
        return ((x_ * 8 + zl) * 2 + core_, y_ * 2 + zh)

    row_up, row_down = lax.rem(row + n_row - 1, n_row), lax.rem(row + 1, n_row)
    col_left, col_right = lax.rem(col + n_col - 1, n_col), lax.rem(col + 1, n_col)
    up, down, lft, rgt = (row_up, col), (row_down, col), (row, col_left), (row, col_right)
    up_left, down_right = (row_up, col_left), (row_down, col_right)
    partner = at(x, y, z_lo, z_hi, 1 - core)
    xy_peers = [(_xor(x, k // 4), _xor(y, k % 4)) for k in range(16)]
    za_peers = [at(x, y, (z_lo // 4) * 4 + _xor(lax.rem(z_lo, 4), k), z_hi, core) for k in range(4)]
    zb_peers = [at(x, y, lax.rem(z_lo + 4 * (k % 2), 8), z_hi if k < 2 else 1 - z_hi, core) for k in range(4)]
    peers = [up, down, lft, rgt, partner, up_left, down_right]
    peers += [at(px, py, z_lo, z_hi, core) for px, py in xy_peers[1:]]
    peers += za_peers[1:] + zb_peers[1:]
    barrier = pltpu.get_barrier_semaphore()
    for peer in peers:
        pl.semaphore_signal(barrier, inc=1, device_id=peer, device_id_type=MESH)

    loads = [
        pltpu.make_async_copy(obj, own, local.at[0]),
        pltpu.make_async_copy(probe_hbm, probe, local.at[1]),
        pltpu.make_async_copy(meas_hbm, meas, local.at[2]),
        pltpu.make_async_copy(tab_hbm, tab, local.at[3]),
    ]
    for load in loads:
        load.start()

    def remote(src, dst, s, r, to):
        return pltpu.make_async_remote_copy(
            src_ref=src, dst_ref=dst, send_sem=s, recv_sem=r, device_id=to, device_id_type=MESH
        )

    def send(src, dst, s, r, to):
        copy = remote(src, dst, s, r, to)
        copy.start()
        return copy

    pl.semaphore_wait(barrier, len(peers))

    def part(ref, i):
        return ref.at[i // SPLIT, pl.ds((i % SPLIT) * (W // SPLIT), W // SPLIT)]

    def send_left(i):
        return send(part(obj, i), part(right, i), fc_s.at[i], fc_r.at[i], lft)

    f_col = [send_left(i) for i in range(AHEAD)]
    f_row = [send(obj.at[p], below.at[p], fr_s.at[p], fr_r.at[p], up) for p in range(4)]
    f_diag = [remote(part(right, i), part(diag, i), fd_s.at[i], fd_r.at[i], up) for i in range(PARTS)]

    @pl.when(first)
    def _():
        for i in range(PARTS):
            send(part(obj, i), part(diag, i), fd_s.at[i], fd_r.at[i], up_left)

    def pass_on(i):
        f_col[i].wait_recv()

        @pl.when(jnp.logical_not(first))
        def _():
            f_diag[i].start()

        if i + AHEAD < PARTS:
            f_col[i].wait_send()
            f_col.append(send_left(i + AHEAD))

    rows_of = lax.broadcasted_iota(jnp.int32, (W, W), 0)
    cols_of = lax.broadcasted_iota(jnp.int32, (W, W), 1)
    corners = [(offs[0, s], offs[1, s]) for s in range(CAP)]
    in_own_row = [rows_of >= r for r, _ in corners]
    in_own_col = [cols_of >= c for _, c in corners]

    for load in loads:
        load.wait()
    waves = [
        tuple(pltpu.roll(pltpu.roll(probe[j], r, 0), c, 1) for j in range(2)) for r, c in corners
    ]

    def window(p, s):
        top = jnp.where(in_own_col[s], own[p], right[p])
        low = jnp.where(in_own_col[s], below[p], diag[p])
        return jnp.where(in_own_row[s], top, low)

    def arrive(p):
        f_row[p].wait_recv()
        for i in range(p * SPLIT, (p + 1) * SPLIT):
            f_diag[i].wait_recv()

    early = 2 * SPLIT + 1
    for i in range(early):
        pass_on(i)
    arrive(0)
    arrive(1)
    patch1 = [(window(0, s), window(1, s)) for s in range(CAP)]
    moved = _two_sided([_mul(waves[s], patch1[s]) for s in range(CAP)], tab.at[0], False)
    for i in range(early, PARTS):
        pass_on(i)
    arrive(2)
    arrive(3)
    patch2 = [(window(2, s), window(3, s)) for s in range(CAP)]
    far = _two_sided([_mul(moved[s], patch2[s]) for s in range(CAP)], tab.at[1], False)
    live_count = cnt[0]
    back = []
    for s in range(CAP):
        re, im = far[s]
        live = jnp.where(live_count > s, 2.0, 0.0).astype(F32)
        excess = (re * re + im * im - meas[s]) * live
        back.append((re * excess, im * excess))
    back = _two_sided(back, tab.at[1], True)

    def spread(p, grads):
        parts = [jnp.zeros((W, W), F32)] * 4
        for s in range(CAP):
            top = jnp.where(in_own_row[s], grads[s], 0.0)
            low = jnp.where(in_own_row[s], 0.0, grads[s])
            parts[0] += jnp.where(in_own_col[s], top, 0.0)
            parts[1] += jnp.where(in_own_col[s], 0.0, top)
            parts[2] += jnp.where(in_own_col[s], low, 0.0)
            parts[3] += jnp.where(in_own_col[s], 0.0, low)
        g_own[p], g_right[p], g_below[p], g_diag[p] = parts

    b_diag = [remote(g_diag.at[p], r_diag.at[p], bd_s.at[p], bd_r.at[p], down) for p in range(4)]
    b_below, b_col = [None] * 4, [None] * 4

    def send_diag(p):
        @pl.when(jnp.logical_not(last))
        def _():
            b_diag[p].start()

        @pl.when(last)
        def _():
            send(g_diag.at[p], r_diag.at[p], bd_s.at[p], bd_r.at[p], down_right)

    def send_below(p):
        b_below[p] = send(g_below.at[p], r_below.at[p], bb_s.at[p], bb_r.at[p], down)

    def send_right(p):
        @pl.when(jnp.logical_not(first))
        def _():
            b_diag[p].wait_recv()
            g_right[p] += r_diag[p]

        b_col[p] = send(g_right.at[p], r_right.at[p], bc_s.at[p], bc_r.at[p], rgt)

    grads = [_mul_conj(back[s], moved[s]) for s in range(CAP)]
    for j in range(2):
        spread(2 + j, [g[j] for g in grads])
        send_diag(2 + j)
    back = _two_sided([_mul_conj(back[s], patch2[s]) for s in range(CAP)], tab.at[0], True)
    grads = [_mul_conj(back[s], waves[s]) for s in range(CAP)]
    for j in range(2):
        spread(j, [g[j] for g in grads])
        send_diag(j)
    probe_grads = [_mul_conj(back[s], patch1[s]) for s in range(CAP)]
    for j in range(2):
        total = jnp.zeros((W, W), F32)
        for s, (r, c) in enumerate(corners):
            total += pltpu.roll(pltpu.roll(probe_grads[s][j], lax.rem(W - r, W), 0), lax.rem(W - c, W), 1)
        gp[j] = total

    to_core = send(gp.at[1 - core], core_in, core_s, core_r, partner)
    send_right(2)
    to_core.wait_recv()
    gp[core] += core_in[...]
    mine = pl.multiple_of((x * 4 + y) * 8, 8)
    to_xy = []
    for k in (1, 2, 3, 4, 5, 6, 7, 8, 9, 10, 11, 12, 13, 14, 15):
        px, py = xy_peers[k]
        start = pl.multiple_of((px * 4 + py) * 8, 8)
        to_xy.append(send(gp.at[core, pl.ds(start, 8)], xy_in.at[k], xy_s.at[k], xy_r.at[k], at(px, py, z_lo, z_hi, core)))
    total = gp[core, pl.ds(mine, 8)]
    for k in range(1, 16):
        to_xy[k - 1].wait_recv()
    for k in range(1, 16):
        total += xy_in[k]
    z_in[0] = total
    to_z = [send(z_in.at[0], z_in.at[k], z_s.at[k], z_r.at[k], za_peers[k]) for k in range(1, 4)]
    send_right(3)
    for copy in to_z[:3]:
        copy.wait_recv()
    z_in[4] = (z_in[0] + z_in[1]) + (z_in[2] + z_in[3])
    to_z += [send(z_in.at[4], z_in.at[4 + k], z_s.at[4 + k], z_r.at[4 + k], zb_peers[k]) for k in range(1, 4)]
    for p in (2, 3, 0, 1):
        send_below(p)
    for copy in to_z[3:]:
        copy.wait_recv()
    total = (z_in[4] + z_in[5]) + (z_in[6] + z_in[7])
    plane[core, pl.ds(mine, 8)] = total * (1.0 / math.sqrt(n_row * n_col * CAP))
    send_right(0)
    send_right(1)
    to_ag = []
    for k in (1, 2, 3, 4, 5, 6, 7, 8, 9, 10, 11, 12, 13, 14, 15):
        px, py = xy_peers[k]
        held = plane.at[core, pl.ds(mine, 8)]
        to_ag.append(send(held, held, ag_s.at[k], ag_r.at[k], at(px, py, z_lo, z_hi, core)))
    for copy in to_ag:
        copy.wait_recv()
    to_cg = send(plane.at[core], plane.at[core], cg_s, cg_r, partner)

    for p in (2, 3, 0, 1):
        b_below[p].wait_recv()
        g_own[p] += r_below[p]

        @pl.when(first)
        def _():
            b_diag[p].wait_recv()
            g_own[p] += r_diag[p]

    for p in (2, 3, 0, 1):
        b_col[p].wait_recv()
        out[p] = g_own[p] + r_right[p]
    to_cg.wait_recv()
    pout[...] = plane[...]
    sent = f_col[PARTS - AHEAD :] + f_row + f_diag + b_below + b_diag + b_col
    for copy in sent + to_xy + to_z + to_ag + [to_core, to_cg]:
        copy.wait_send()


def _per_device(n_row, n_col, object_slices, probe_field, measured, offsets, counts):
    obj = object_slices.reshape(4, W, W)
    dma = pltpu.SemaphoreType.DMA
    tile = pltpu.VMEM((4, W, W), F32)
    any_, vmem, smem = (pl.BlockSpec(memory_space=m) for m in (pl.ANY, pltpu.VMEM, pltpu.SMEM))
    out, pout = pl.pallas_call(
        functools.partial(_kernel, n_row, n_col),
        out_shape=(jax.ShapeDtypeStruct((4, W, W), F32), jax.ShapeDtypeStruct((2, W, W), F32)),
        in_specs=[smem, smem, any_, any_, any_, any_],
        out_specs=(vmem, vmem),
        scratch_shapes=[tile] * 11
        + [
            pltpu.VMEM((2, W, W), F32),
            pltpu.VMEM((CAP, W, W), F32),
            pltpu.VMEM((2, 6, W, W), BF16),
            pltpu.VMEM((2, W, W), F32),
            pltpu.VMEM((W, W), F32),
            pltpu.VMEM((16, 8, W), F32),
            pltpu.VMEM((8, 8, W), F32),
            pltpu.VMEM((2, W, W), F32),
        ]
        + [dma((4,))]
        + [dma((PARTS,))] * 2
        + [dma((4,))] * 2
        + [dma((PARTS,))] * 2
        + [dma((4,))] * 6
        + [dma, dma]
        + [dma((16,))] * 2
        + [dma((8,))] * 2
        + [dma((16,))] * 2
        + [dma, dma],
        compiler_params=pltpu.CompilerParams(
            collective_id=0, has_side_effects=True, vmem_limit_bytes=60 * 1024 * 1024
        ),
    )(offsets.T, counts, obj, probe_field, measured, jnp.asarray(_tables()))
    return out.reshape(object_slices.shape), pout


def solution(mesh):
    in_specs = (
        P(None, None, "row", "col"),
        P(),
        P(("row", "col"), None, None),
        P(("row", "col"), None),
        P(("row", "col")),
    )
    out_specs = (P(None, None, "row", "col"), P())
    return jax.shard_map(
        functools.partial(_per_device, mesh.shape["row"], mesh.shape["col"]),
        mesh=mesh,
        in_specs=in_specs,
        out_specs=out_specs,
        check_vma=False,
    )
```

```python
import functools
import math

import jax
import jax.numpy as jnp
import ml_dtypes
import numpy as np
from jax import lax
from jax.experimental import pallas as pl
from jax.experimental.pallas import tpu as pltpu
from jax.sharding import PartitionSpec as P

PROP = 40.0
W = 128
CAP = 4
SPLIT = 2
PARTS = 4 * SPLIT
AHEAD = 8
MESH = pl.DeviceIdType.MESH
F32 = jnp.float32
BF16 = jnp.bfloat16


def _tables():
    k = np.arange(W)
    dft = np.exp(-2j * np.pi * (np.outer(k, k) % W) / W) / math.sqrt(W)
    freq = np.where(k < W // 2, k, k - W).astype(np.float64)
    h = np.exp(-1j * PROP * freq**2 / (W * W))
    prop = np.conj(dft) @ (h[:, None] * dft)
    out = np.zeros((2, 6, W, W), ml_dtypes.bfloat16)
    for t, table in enumerate((prop, dft)):
        for j, part in enumerate((table.real, table.imag, -table.imag)):
            part = part.astype(np.float32)
            high = part.astype(ml_dtypes.bfloat16)
            out[t, j] = high
            out[t, 3 + j] = (part - high.astype(np.float32)).astype(ml_dtypes.bfloat16)
    return out


def _split(x):
    high = x.astype(BF16)
    return high, (x - high.astype(F32)).astype(BF16)


def _blocks(tab, conj):
    parts = []
    for base in (0, 3):
        re, im, neg = tab[base], tab[base + 1], tab[base + 2]
        if conj:
            im, neg = neg, im
        parts.append(jnp.concatenate([jnp.concatenate([re, im], 1), jnp.concatenate([neg, re], 1)], 0))
    return parts


def _two_sided(fields, tab, conj):
    n = len(fields)
    wh, wl = _blocks(tab, conj)
    vh, vl = _blocks(tab, not conj)
    stacked = jnp.concatenate([jnp.concatenate([re, im], 1) for re, im in fields], 0)
    high, low = _split(stacked)
    y = jnp.dot(
        jnp.concatenate([high, low, high], 1), jnp.concatenate([wh, wh, wl], 0), preferred_element_type=F32
    )
    beside = jnp.concatenate(
        [jnp.concatenate([y[s * W : (s + 1) * W, :W], y[s * W : (s + 1) * W, W:]], 0) for s in range(n)], 1
    )
    high, low = _split(beside)
    z = jnp.dot(
        jnp.concatenate([vh, vh, vl], 1), jnp.concatenate([high, low, high], 0), preferred_element_type=F32
    )
    return [(z[:W, s * W : (s + 1) * W], z[W:, s * W : (s + 1) * W]) for s in range(n)]


def _mul(a, b):
    return a[0] * b[0] - a[1] * b[1], a[0] * b[1] + a[1] * b[0]


def _mul_conj(a, b):
    return a[0] * b[0] + a[1] * b[1], a[1] * b[0] - a[0] * b[1]


def _xor(i, k):
    if k == 0:
        return i
    if k == 1:
        return i + 1 - 2 * lax.rem(i, 2)
    if k == 2:
        return lax.rem(i + 2, 4)
    return 3 - i


def _kernel(
    n_row, n_col, offs, cnt, obj, probe_hbm, meas_hbm, tab_hbm, out, pout,
    own, right, below, diag, g_own, g_right, g_below, g_diag, r_right, r_below, r_diag,
    probe, meas, tab, gp, core_in, xy_in, z_in, plane,
    local, fc_s, fc_r, fr_s, fr_r, fd_s, fd_r, bb_s, bb_r, bd_s, bd_r, bc_s, bc_r,
    core_s, core_r, xy_s, xy_r, z_s, z_r, ag_s, ag_r, cg_s, cg_r,
):
    row, col = lax.axis_index("row"), lax.axis_index("col")
    core = lax.rem(row, 2)
    z_lo = lax.rem(row // 2, 8)
    x = row // 16
    z_hi = lax.rem(col, 2)
    y = col // 2
    first, last = lax.rem(row, 16) == 0, lax.rem(row, 16) == 15

    def at(x_, y_, zl, zh, core_):
        return ((x_ * 8 + zl) * 2 + core_, y_ * 2 + zh)

    row_up, row_down = lax.rem(row + n_row - 1, n_row), lax.rem(row + 1, n_row)
    col_left, col_right = lax.rem(col + n_col - 1, n_col), lax.rem(col + 1, n_col)
    up, down, lft, rgt = (row_up, col), (row_down, col), (row, col_left), (row, col_right)
    up_left, down_right = (row_up, col_left), (row_down, col_right)
    partner = at(x, y, z_lo, z_hi, 1 - core)
    xy_peers = [(_xor(x, k // 4), _xor(y, k % 4)) for k in range(16)]
    za_peers = [at(x, y, (z_lo // 4) * 4 + _xor(lax.rem(z_lo, 4), k), z_hi, core) for k in range(4)]
    zb_peers = [at(x, y, lax.rem(z_lo + 4 * (k % 2), 8), z_hi if k < 2 else 1 - z_hi, core) for k in range(4)]
    peers = [up, down, lft, rgt, partner, up_left, down_right]
    peers += [at(px, py, z_lo, z_hi, core) for px, py in xy_peers[1:]]
    peers += za_peers[1:] + zb_peers[1:]
    barrier = pltpu.get_barrier_semaphore()
    for peer in peers:
        pl.semaphore_signal(barrier, inc=1, device_id=peer, device_id_type=MESH)

    loads = [
        pltpu.make_async_copy(obj, own, local.at[0]),
        pltpu.make_async_copy(probe_hbm, probe, local.at[1]),
        pltpu.make_async_copy(meas_hbm, meas, local.at[2]),
        pltpu.make_async_copy(tab_hbm, tab, local.at[3]),
    ]
    for load in loads:
        load.start()

    def remote(src, dst, s, r, to):
        return pltpu.make_async_remote_copy(
            src_ref=src, dst_ref=dst, send_sem=s, recv_sem=r, device_id=to, device_id_type=MESH
        )

    def send(src, dst, s, r, to):
        copy = remote(src, dst, s, r, to)
        copy.start()
        return copy

    pl.semaphore_wait(barrier, len(peers))

    def part(ref, i):
        return ref.at[i // SPLIT, pl.ds((i % SPLIT) * (W // SPLIT), W // SPLIT)]

    def send_left(i):
        return send(part(obj, i), part(right, i), fc_s.at[i], fc_r.at[i], lft)

    f_col = [send_left(i) for i in range(AHEAD)]
    f_row = [send(obj.at[p], below.at[p], fr_s.at[p], fr_r.at[p], up) for p in range(4)]
    f_diag = [remote(part(right, i), part(diag, i), fd_s.at[i], fd_r.at[i], up) for i in range(PARTS)]

    @pl.when(first)
    def _():
        for i in range(PARTS):
            send(part(obj, i), part(diag, i), fd_s.at[i], fd_r.at[i], up_left)

    def pass_on(i):
        f_col[i].wait_recv()

        @pl.when(jnp.logical_not(first))
        def _():
            f_diag[i].start()

        if i + AHEAD < PARTS:
            f_col[i].wait_send()
            f_col.append(send_left(i + AHEAD))

    rows_of = lax.broadcasted_iota(jnp.int32, (W, W), 0)
    cols_of = lax.broadcasted_iota(jnp.int32, (W, W), 1)
    corners = [(offs[0, s], offs[1, s]) for s in range(CAP)]
    in_own_row = [rows_of >= r for r, _ in corners]
    in_own_col = [cols_of >= c for _, c in corners]

    for load in loads:
        load.wait()
    waves = [
        tuple(pltpu.roll(pltpu.roll(probe[j], r, 0), c, 1) for j in range(2)) for r, c in corners
    ]

    def window(p, s):
        top = jnp.where(in_own_col[s], own[p], right[p])
        low = jnp.where(in_own_col[s], below[p], diag[p])
        return jnp.where(in_own_row[s], top, low)

    def arrive(p):
        f_row[p].wait_recv()
        for i in range(p * SPLIT, (p + 1) * SPLIT):
            f_diag[i].wait_recv()

    early = 2 * SPLIT + 1
    for i in range(early):
        pass_on(i)
    arrive(0)
    arrive(1)
    patch1 = [(window(0, s), window(1, s)) for s in range(CAP)]
    moved = _two_sided([_mul(waves[s], patch1[s]) for s in range(CAP)], tab.at[0], False)
    for i in range(early, PARTS):
        pass_on(i)
    arrive(2)
    arrive(3)
    patch2 = [(window(2, s), window(3, s)) for s in range(CAP)]
    far = _two_sided([_mul(moved[s], patch2[s]) for s in range(CAP)], tab.at[1], False)
    live_count = cnt[0]
    back = []
    for s in range(CAP):
        re, im = far[s]
        live = jnp.where(live_count > s, 2.0, 0.0).astype(F32)
        excess = (re * re + im * im - meas[s]) * live
        back.append((re * excess, im * excess))
    back = _two_sided(back, tab.at[1], True)

    def spread(p, grads):
        parts = [jnp.zeros((W, W), F32)] * 4
        for s in range(CAP):
            top = jnp.where(in_own_row[s], grads[s], 0.0)
            low = jnp.where(in_own_row[s], 0.0, grads[s])
            parts[0] += jnp.where(in_own_col[s], top, 0.0)
            parts[1] += jnp.where(in_own_col[s], 0.0, top)
            parts[2] += jnp.where(in_own_col[s], low, 0.0)
            parts[3] += jnp.where(in_own_col[s], 0.0, low)
        g_own[p], g_right[p], g_below[p], g_diag[p] = parts

    b_diag = [remote(g_diag.at[p], r_diag.at[p], bd_s.at[p], bd_r.at[p], down) for p in range(4)]
    b_below, b_col = [None] * 4, [None] * 4

    def send_diag(p):
        @pl.when(jnp.logical_not(last))
        def _():
            b_diag[p].start()

        @pl.when(last)
        def _():
            send(g_diag.at[p], r_diag.at[p], bd_s.at[p], bd_r.at[p], down_right)

    def send_below(p):
        b_below[p] = send(g_below.at[p], r_below.at[p], bb_s.at[p], bb_r.at[p], down)

    def send_right(p):
        @pl.when(jnp.logical_not(first))
        def _():
            b_diag[p].wait_recv()
            g_right[p] += r_diag[p]

        b_col[p] = send(g_right.at[p], r_right.at[p], bc_s.at[p], bc_r.at[p], rgt)

    grads = [_mul_conj(back[s], moved[s]) for s in range(CAP)]
    for j in range(2):
        spread(2 + j, [g[j] for g in grads])
        send_diag(2 + j)
    back = _two_sided([_mul_conj(back[s], patch2[s]) for s in range(CAP)], tab.at[0], True)
    grads = [_mul_conj(back[s], waves[s]) for s in range(CAP)]
    for j in range(2):
        spread(j, [g[j] for g in grads])
        send_diag(j)
    probe_grads = [_mul_conj(back[s], patch1[s]) for s in range(CAP)]
    for j in range(2):
        total = jnp.zeros((W, W), F32)
        for s, (r, c) in enumerate(corners):
            total += pltpu.roll(pltpu.roll(probe_grads[s][j], lax.rem(W - r, W), 0), lax.rem(W - c, W), 1)
        gp[j] = total

    to_core = send(gp.at[1 - core], core_in, core_s, core_r, partner)
    send_right(2)
    to_core.wait_recv()
    gp[core] += core_in[...]
    mine = pl.multiple_of((x * 4 + y) * 8, 8)
    to_xy = []
    for k in (1, 2, 3, 4, 5, 6, 7, 8, 9, 10, 11, 12, 13, 14, 15):
        px, py = xy_peers[k]
        start = pl.multiple_of((px * 4 + py) * 8, 8)
        to_xy.append(send(gp.at[core, pl.ds(start, 8)], xy_in.at[k], xy_s.at[k], xy_r.at[k], at(px, py, z_lo, z_hi, core)))
    total = gp[core, pl.ds(mine, 8)]
    for k in range(1, 16):
        to_xy[k - 1].wait_recv()
    for k in range(1, 16):
        total += xy_in[k]
    z_in[0] = total
    to_z = [send(z_in.at[0], z_in.at[k], z_s.at[k], z_r.at[k], za_peers[k]) for k in range(1, 4)]
    send_right(3)
    for copy in to_z[:3]:
        copy.wait_recv()
    z_in[4] = (z_in[0] + z_in[1]) + (z_in[2] + z_in[3])
    to_z += [send(z_in.at[4], z_in.at[4 + k], z_s.at[4 + k], z_r.at[4 + k], zb_peers[k]) for k in range(1, 4)]
    for p in (2, 3, 0, 1):
        send_below(p)
    for copy in to_z[3:]:
        copy.wait_recv()
    total = (z_in[4] + z_in[5]) + (z_in[6] + z_in[7])
    plane[core, pl.ds(mine, 8)] = total * (1.0 / math.sqrt(n_row * n_col * CAP))
    to_ag = []
    for k in (1, 2, 3, 4, 5, 6, 7, 8, 9, 10, 11, 12, 13, 14, 15):
        px, py = xy_peers[k]
        held = plane.at[core, pl.ds(mine, 8)]
        to_ag.append(send(held, held, ag_s.at[k], ag_r.at[k], at(px, py, z_lo, z_hi, core)))
    send_right(0)
    send_right(1)
    for copy in to_ag:
        copy.wait_recv()
    to_cg = send(plane.at[core], plane.at[core], cg_s, cg_r, partner)

    for p in (2, 3, 0, 1):
        b_below[p].wait_recv()
        g_own[p] += r_below[p]

        @pl.when(first)
        def _():
            b_diag[p].wait_recv()
            g_own[p] += r_diag[p]

    for p in (2, 3, 0, 1):
        b_col[p].wait_recv()
        out[p] = g_own[p] + r_right[p]
    to_cg.wait_recv()
    pout[...] = plane[...]
    sent = f_col[PARTS - AHEAD :] + f_row + f_diag + b_below + b_diag + b_col
    for copy in sent + to_xy + to_z + to_ag + [to_core, to_cg]:
        copy.wait_send()


def _per_device(n_row, n_col, object_slices, probe_field, measured, offsets, counts):
    obj = object_slices.reshape(4, W, W)
    dma = pltpu.SemaphoreType.DMA
    tile = pltpu.VMEM((4, W, W), F32)
    any_, vmem, smem = (pl.BlockSpec(memory_space=m) for m in (pl.ANY, pltpu.VMEM, pltpu.SMEM))
    out, pout = pl.pallas_call(
        functools.partial(_kernel, n_row, n_col),
        out_shape=(jax.ShapeDtypeStruct((4, W, W), F32), jax.ShapeDtypeStruct((2, W, W), F32)),
        in_specs=[smem, smem, any_, any_, any_, any_],
        out_specs=(vmem, vmem),
        scratch_shapes=[tile] * 11
        + [
            pltpu.VMEM((2, W, W), F32),
            pltpu.VMEM((CAP, W, W), F32),
            pltpu.VMEM((2, 6, W, W), BF16),
            pltpu.VMEM((2, W, W), F32),
            pltpu.VMEM((W, W), F32),
            pltpu.VMEM((16, 8, W), F32),
            pltpu.VMEM((8, 8, W), F32),
            pltpu.VMEM((2, W, W), F32),
        ]
        + [dma((4,))]
        + [dma((PARTS,))] * 2
        + [dma((4,))] * 2
        + [dma((PARTS,))] * 2
        + [dma((4,))] * 6
        + [dma, dma]
        + [dma((16,))] * 2
        + [dma((8,))] * 2
        + [dma((16,))] * 2
        + [dma, dma],
        compiler_params=pltpu.CompilerParams(
            collective_id=0, has_side_effects=True, vmem_limit_bytes=60 * 1024 * 1024
        ),
    )(offsets.T, counts, obj, probe_field, measured, jnp.asarray(_tables()))
    return out.reshape(object_slices.shape), pout


def solution(mesh):
    in_specs = (
        P(None, None, "row", "col"),
        P(),
        P(("row", "col"), None, None),
        P(("row", "col"), None),
        P(("row", "col")),
    )
    out_specs = (P(None, None, "row", "col"), P())
    return jax.shard_map(
        functools.partial(_per_device, mesh.shape["row"], mesh.shape["col"]),
        mesh=mesh,
        in_specs=in_specs,
        out_specs=out_specs,
        check_vma=False,
    )
```
